1024 devices in a mesh: row: 32 (over x, z_hi, core), col: 32 (over y, z_lo).
Axes of the slice: x: 8, y: 8, z: 8 (z_hi: 2, z_lo: 4; z = z_hi * 4 + z_lo), core: 2. Of those that a mesh axis runs over, the one named last changes fastest.
Arguments:
- a_blocks: bfloat16 [32, 32, 8, 256, 256], P('row', 'col'), may hold values from -0.375 to 0.375
- a_rows: int32 [32, 32, 2, 4], P('row', 'col'), may hold values from -1 to 1, as said below
- b_blocks: bfloat16 [32, 32, 8, 256, 256], P('row', 'col'), may hold values from -6 to 6
- b_cols: int32 [32, 32, 2, 4], P('row', 'col'), may hold values from -1 to 1, as said below
- c_pattern: int32 [32, 32, 3], P('row', 'col'), may hold values from 0 to 3, as said below
Outputs:
- c_blocks: bfloat16 [32, 32, 3, 256, 256], P('row', 'col')
The draws below stay inside these ranges and needn't reach their ends.
Inputs may be any that keep to these rules, and one draw needn't show every extreme that they name: `a_rows`: each panel has exactly 6 slots that are not -1. `b_cols`: each panel has exactly 6 slots that are not -1. `c_pattern`: the entries of one panel's pattern are distinct.
All inputs are finite; a program needn't handle non-finite values.
Results may differ from the reference program's by a relative error of at most 0.001.
Values may be sent and summed in bfloat16 or wider, within the bound.
A program may use at most 64 MiB of HBM per device.

```python
import jax
import jax.numpy as jnp
from jax import lax

BS = 256
PB = 2
MA = 4
SLOTS = 8
LIVE = 6
CB = 3
N_ROW = 32
N_COL = 32


def slot_labels(key):
    live_key, value_key = jax.random.split(key)
    scores = jax.random.randint(live_key, (SLOTS,), 0, 1 << 20) * SLOTS + jnp.arange(SLOTS)
    order = jnp.argsort(scores)
    ranks = jnp.argsort(order)
    values = jax.random.randint(value_key, (SLOTS,), 0, PB)
    labels = jnp.where(ranks < LIVE, values, -1)
    return labels.reshape(PB, MA).astype(jnp.int32)


def draw_a_rows(key, part):
    key = jax.random.fold_in(key, 11)
    keys = jax.random.split(key, N_ROW * N_COL)
    labels = jax.vmap(slot_labels)(keys)
    return labels.reshape(N_ROW, N_COL, PB, MA)


def draw_b_cols(key, part):
    key = jax.random.fold_in(key, 23)
    keys = jax.random.split(key, N_ROW * N_COL)
    labels = jax.vmap(slot_labels)(keys)
    return labels.reshape(N_ROW, N_COL, PB, MA)


def pattern_one(key):
    total = PB * PB
    scores = jax.random.randint(key, (total,), 0, 1 << 20) * total + jnp.arange(total)
    order = jnp.argsort(scores)
    return order[:CB].astype(jnp.int32)


def draw_c_pattern(key, part):
    key = jax.random.fold_in(key, 37)
    keys = jax.random.split(key, N_ROW * N_COL)
    picks = jax.vmap(pattern_one)(keys)
    return picks.reshape(N_ROW, N_COL, CB)


def block_levels(rng, extent, shards, least, high):
    def one(axis_at, parts):
        draws = jax.random.uniform(jax.random.fold_in(jax.random.fold_in(rng, 6), axis_at), (parts,), jnp.float32, least / len(shards), high / len(shards))
        return jnp.repeat(jnp.exp(draws), extent[axis_at] // parts).reshape((-1,) + (1,) * (len(extent) - axis_at - 1))

    loudness = one(*shards[0])
    for cut in shards[1:]:
        loudness = loudness * one(*cut)
    return loudness


def noise(rng, shape, deviation, limit, cuts=(), kind=jnp.bfloat16):
    factor_of = block_levels(rng, shape, cuts, -0.22, 0.18) if cuts else 1.0
    drawn = jax.random.normal(rng, shape, jnp.float32) * deviation * factor_of
    return jnp.minimum(jnp.maximum(drawn, -limit), limit).astype(kind)


def setup_inputs(seed: int = 0) -> dict:
    seeds = jax.random.split(jax.random.key(seed), 6)
    return {
        "a_blocks": noise(seeds[0], (N_ROW, N_COL, SLOTS, BS, BS), BS ** -0.5, 0.375, ((0, 32), (1, 32))),
        "a_rows": draw_a_rows(jax.random.fold_in(seeds[5], 71), 0),
        "b_blocks": noise(seeds[2], (N_ROW, N_COL, SLOTS, BS, BS), 1.0, 6.0, ((0, 32), (1, 32))),
        "b_cols": draw_b_cols(jax.random.fold_in(seeds[5], 71), 0),
        "c_pattern": draw_c_pattern(jax.random.fold_in(seeds[5], 71), 0),
    }


def panel_terms(a_vals, rows, b_vals, cols, pattern):
    panel_rows = rows.shape[0]
    width = rows.shape[1]
    size = a_vals.shape[-1]
    left = a_vals.reshape(panel_rows, width, size, size).astype(jnp.float32)
    right = b_vals.reshape(panel_rows, width, size, size).astype(jnp.float32)
    products = jnp.einsum("kmxy,knyz->kmnxz", left, right)
    target = rows[:, :, None] * panel_rows + cols[:, None, :]
    valid = (rows[:, :, None] >= 0) & (cols[:, None, :] >= 0)
    target = jnp.where(valid, target, -1).reshape(-1)
    select = (pattern[:, None] == target[None, :]).astype(jnp.float32)
    flat = products.reshape(-1, size, size)
    return jnp.einsum("cq,qxz->cxz", select, flat, precision=lax.Precision.HIGHEST)


def reference(a_blocks, a_rows, b_blocks, b_cols, c_pattern):
    a_next = jnp.roll(a_blocks, -1, axis=0)
    rows_next = jnp.roll(a_rows, -1, axis=0)
    b_next = jnp.roll(b_blocks, -1, axis=1)
    cols_next = jnp.roll(b_cols, -1, axis=1)

    def grid_row(items):
        first = jax.vmap(panel_terms)(items[0], items[1], items[2], items[3], items[4])
        second = jax.vmap(panel_terms)(items[5], items[6], items[7], items[8], items[4])
        return (first + second).astype(jnp.bfloat16)

    return lax.map(grid_row, (a_blocks, a_rows, b_blocks, b_cols, c_pattern, a_next, rows_next, b_next, cols_next))
```

```python
import jax
import jax.numpy as jnp
from jax import lax
from jax.experimental import pallas as pl
from jax.experimental.pallas import tpu as pltpu
from jax.sharding import PartitionSpec as P

MESH = pl.DeviceIdType.MESH
TINY = 1.2e-34
TOP = 32767.0


def split(value):
    high = value.astype(jnp.bfloat16)
    low = (value - high.astype(jnp.float32)).astype(jnp.bfloat16)
    return high, low


def kernel(
    a_hbm, rows, b_hbm, cols, pattern, out,
    a_in, b_in, a_send, b_send, a_got, b_got, a_scale, b_scale, a_scale_got, b_scale_got,
    a_high, a_low, b_high, b_low, total,
    load_sem, a_send_sem, a_recv_sem, b_send_sem, b_recv_sem,
):
    n_row, n_col = lax.axis_size("row"), lax.axis_size("col")
    r, c = lax.axis_index("row"), lax.axis_index("col")
    panel_rows, width = rows.shape[2], rows.shape[3]
    size = a_in.shape[-1]

    loads = []
    for k in range(panel_rows):
        part = pl.ds(k * width, width)
        for n, (source, target) in enumerate(((a_hbm, a_in), (b_hbm, b_in))):
            copy = pltpu.make_async_copy(source.at[0, 0, part], target.at[part], load_sem.at[n, k])
            copy.start()
            loads.append(copy)

    barrier = pltpu.get_barrier_semaphore()
    below = lax.rem(r + n_row - 1, n_row)
    left = lax.rem(c + n_col - 1, n_col)
    pl.semaphore_signal(barrier, inc=1, device_id=(lax.rem(r + 1, n_row), c), device_id_type=MESH)
    pl.semaphore_signal(barrier, inc=1, device_id=(r, lax.rem(c + 1, n_col)), device_id_type=MESH)

    def send(source, target, sems, at, device):
        return pltpu.make_async_remote_copy(
            src_ref=source, dst_ref=target, send_sem=sems[0].at[at], recv_sem=sems[1].at[at],
            device_id=device, device_id_type=MESH,
        )

    def coded(value, queue, scale, at):
        peak = jnp.maximum(jnp.max(jnp.abs(value), axis=0, keepdims=True), TINY)
        queue[at] = jnp.round(value * (TOP / peak)).astype(jnp.int32).astype(jnp.int16)
        scale[pl.ds(at, 1), :] = peak * (1.0 / TOP)

    def summed(labels, blocks, k, want):
        value = None
        for m in range(width):
            weight = (labels[0, 0, k, m] == want).astype(jnp.float32)
            term = blocks[k * width + m].astype(jnp.float32) * weight
            value = term if value is None else value + term
        return value

    copies = []
    a_sems, b_sems = (a_send_sem, a_recv_sem), (b_send_sem, b_recv_sem)
    a_to, b_to = (below, c), (r, left)
    for k in range(panel_rows):
        span = pl.ds(k * size, size)
        loads[2 * k].wait()
        for i in range(panel_rows):
            at = k * panel_rows + i
            value = summed(rows, a_in, k, i)
            coded(value, a_send, a_scale, at)
            a_high[i, :, span], a_low[i, :, span] = split(value)
            if k == 0 and i == 0:
                pl.semaphore_wait(barrier, 2)
            copy = send(a_send.at[at], a_got.at[at], a_sems, at, a_to)
            copy.start()
            copies.append(copy)
        loads[2 * k + 1].wait()
        for j in range(panel_rows):
            at = k * panel_rows + j
            value = summed(cols, b_in, k, j)
            coded(value, b_send, b_scale, at)
            b_high[j, span, :], b_low[j, span, :] = split(value)
            copy = send(b_send.at[at], b_got.at[at], b_sems, at, b_to)
            copy.start()
            copies.append(copy)
    last = panel_rows * panel_rows
    for copy in (
        send(a_scale, a_scale_got, a_sems, last, a_to),
        send(b_scale, b_scale_got, b_sems, last, b_to),
    ):
        copy.start()
        copies.append(copy)

    def product(target):
        i, j = target >> 1, target & 1
        ah, al, bh, bl = a_high[i], a_low[i], b_high[j], b_low[j]
        dot = lambda x, y: jnp.dot(x, y, preferred_element_type=jnp.float32)
        return dot(ah, bh) + (dot(ah, bl) + dot(al, bh) + dot(al, bl))

    kept = pattern.shape[2]
    for n in range(kept):
        total[n] = product(pattern[0, 0, n])

    for copy in copies:
        copy.wait_send()
    for copy in copies:
        copy.wait_recv()
    for k in range(panel_rows):
        span = pl.ds(k * size, size)
        for i in range(panel_rows):
            at = k * panel_rows + i
            value = a_got[at].astype(jnp.int32).astype(jnp.float32) * a_scale_got[pl.ds(at, 1), :]
            a_high[i, :, span], a_low[i, :, span] = split(value)
            value = b_got[at].astype(jnp.int32).astype(jnp.float32) * b_scale_got[pl.ds(at, 1), :]
            b_high[i, span, :], b_low[i, span, :] = split(value)
    for n in range(kept):
        out[0, 0, n] = (total[n] + product(pattern[0, 0, n])).astype(out.dtype)


def body(a_blocks, a_rows, b_blocks, b_cols, c_pattern):
    slots, size = a_blocks.shape[2], a_blocks.shape[-1]
    panel_rows = a_rows.shape[2]
    kept = c_pattern.shape[2]
    groups = panel_rows * panel_rows
    smem = pl.BlockSpec(memory_space=pltpu.SMEM)
    anywhere = pl.BlockSpec(memory_space=pl.ANY)
    bf16, f32 = jnp.bfloat16, jnp.float32
    depth = panel_rows * size
    queue = pltpu.VMEM((groups, size, size), jnp.int16)
    scale = pltpu.VMEM((8, size), f32)
    sems = pltpu.SemaphoreType.DMA((groups + 1,))
    return pl.pallas_call(
        kernel,
        out_shape=jax.ShapeDtypeStruct((1, 1, kept, size, size), bf16),
        in_specs=[anywhere, smem, anywhere, smem, smem],
        out_specs=pl.BlockSpec(memory_space=pltpu.VMEM),
        scratch_shapes=[
            pltpu.VMEM((slots, size, size), bf16), pltpu.VMEM((slots, size, size), bf16),
            queue, queue, queue, queue, scale, scale, scale, scale,
            pltpu.VMEM((panel_rows, size, depth), bf16), pltpu.VMEM((panel_rows, size, depth), bf16),
            pltpu.VMEM((panel_rows, depth, size), bf16), pltpu.VMEM((panel_rows, depth, size), bf16),
            pltpu.VMEM((kept, size, size), f32),
            pltpu.SemaphoreType.DMA((2, panel_rows)), sems, sems, sems, sems,
        ],
        compiler_params=pltpu.CompilerParams(
            collective_id=0, has_side_effects=True, vmem_limit_bytes=60 << 20
        ),
        cost_estimate=pl.CostEstimate(flops=64 * 2 * size**3, bytes_accessed=3 << 20, transcendentals=0),
    )(a_blocks, a_rows, b_blocks, b_cols, c_pattern)


def solution(mesh):
    in_specs = (
        P("row", "col", None, None, None),
        P("row", "col", None, None),
        P("row", "col", None, None, None),
        P("row", "col", None, None),
        P("row", "col", None),
    )
    out_specs = P("row", "col", None, None, None)
    return jax.shard_map(body, mesh=mesh, in_specs=in_specs, out_specs=out_specs, check_vma=False)
```

```python
import functools

import jax
import jax.numpy as jnp
from jax import lax
from jax.experimental import pallas as pl
from jax.experimental.pallas import tpu as pltpu
from jax.sharding import PartitionSpec as P

MESH = pl.DeviceIdType.MESH
TINY = 1.2e-34
TOP = 32767.0
RETURNED = 0b0
HOLDS = 0b10110000


def split(value):
    high = value.astype(jnp.bfloat16)
    low = (value - high.astype(jnp.float32)).astype(jnp.bfloat16)
    return high, low


def kernel(
    a_hbm, rows, b_hbm, cols, pattern, out,
    a_in, b_in, a_send, b_send, c_send, a_got, b_got, c_got,
    a_scale, b_scale, c_scale, a_scale_got, b_scale_got, c_scale_got,
    a_high, a_low, b_high, b_low, far_a_high, far_a_low, far_b_high, far_b_low, total,
    load_sem, a_send_sem, b_send_sem, c_send_sem, a_recv_sem, b_recv_sem, c_recv_sem, below_in, left_in, sent,
):
    n_row, n_col = lax.axis_size("row"), lax.axis_size("col")
    r, c = lax.axis_index("row"), lax.axis_index("col")
    panel_rows, width = rows.shape[2], rows.shape[3]
    size = a_in.shape[-1]
    groups = panel_rows * panel_rows
    both, either, no = jnp.logical_and, jnp.logical_or, jnp.logical_not

    core, half, lane = lax.rem(r, 2), lax.rem(lax.div(r, 2), 2), lax.rem(c, 4)
    late = half == 1
    early = no(late)

    def listed(table, half, lane):
        return lax.rem(lax.shift_right_logical(table, half * 4 + lane), 2)

    near, far = core == 1, core == 0
    shift = jnp.where(far, listed(RETURNED, 1 - half, lane), 0)
    is_returned = both(near, listed(RETURNED, half, lane) == 1)
    serves = both(near, listed(RETURNED, half, lax.rem(lane + 3, 4)) == 1)
    holds_b = both(late, listed(HOLDS, half, lane) == 1)
    holds_a = both(early, listed(HOLDS, half, lane) == 1)
    takes_a, sends_b = no(is_returned), no(serves)

    c_up, c_left = lax.rem(c + 1, n_col), lax.rem(c + n_col - 1, n_col)
    r_up = lax.rem(r + 1, n_row)
    target = (lax.rem(r + n_row - 1, n_row), lax.rem(c + shift, n_col))
    up, across = (r_up, c), (r_up, c_left)
    right, left = (r, c_up), (r, c_left)

    loads = []
    for k in range(panel_rows):
        part = pl.ds(k * width, width)
        for n, (source, into) in enumerate(((a_hbm, a_in), (b_hbm, b_in))):
            copy = pltpu.make_async_copy(source.at[0, 0, part], into.at[part], load_sem.at[n, k])
            copy.start()
            loads.append(copy)

    barrier = pltpu.get_barrier_semaphore()
    target_later = either(near, early)
    source_later = both(near, early)
    right_later, left_later = lane < 3, lane == 0

    def signal(sem, device):
        pl.semaphore_signal(sem, inc=1, device_id=device, device_id_type=MESH)

    before = 0
    for there, later, device in (
        (takes_a, source_later, up),
        (serves, source_later, across),
        (core >= 0, target_later, target),
        (core >= 0, right_later, right),
        (core >= 0, left_later, left),
    ):
        pl.when(both(there, later))(functools.partial(signal, barrier, device))
        before = before + jnp.where(both(there, no(later)), 1, 0)

    @pl.when(before > 0)
    def _():
        pl.semaphore_wait(barrier, before)

    pl.when(both(takes_a, no(source_later)))(functools.partial(signal, below_in, up))
    pl.when(both(serves, no(source_later)))(functools.partial(signal, below_in, across))
    pl.when(no(right_later))(functools.partial(signal, left_in, right))

    def await_target():
        @pl.when(target_later)
        def _():
            pl.semaphore_wait(below_in, 1)

    def await_left():
        @pl.when(left_later)
        def _():
            pl.semaphore_wait(left_in, 1)

    def send(source, into, send_sem, recv_sem, device):
        return pltpu.make_async_remote_copy(
            src_ref=source, dst_ref=into, send_sem=send_sem, recv_sem=recv_sem,
            device_id=device, device_id_type=MESH,
        )

    def a_copy(at, slot):
        sems = a_send_sem.at[at], a_recv_sem.at[slot, at]
        if at == groups:
            return send(a_scale, a_scale_got.at[slot], *sems, target)
        return send(a_send.at[at], a_got.at[slot, at], *sems, target)

    def b_copy(at):
        sems = b_send_sem.at[at], b_recv_sem.at[at]
        if at == groups:
            return send(b_scale, b_scale_got, *sems, left)
        return send(b_send.at[at], b_got.at[at], *sems, left)

    def c_copy(at):
        sems = c_send_sem.at[at], c_recv_sem.at[at]
        if at == groups:
            return send(c_scale, c_scale_got, *sems, left)
        return send(c_send.at[at], c_got.at[at], *sems, left)

    def each(copy, act, *more):
        for at in range(groups + 1):
            getattr(copy(at, *more), act)()

    def coded(value, queue, scale, at):
        peak = jnp.maximum(jnp.max(jnp.abs(value), axis=0, keepdims=True), TINY)
        queue[at] = jnp.round(value * (TOP / peak)).astype(jnp.int32).astype(jnp.int16)
        scale[pl.ds(at, 1), :] = peak * (1.0 / TOP)

    def decoded(queue, scale, at):
        return queue[at].astype(jnp.int32).astype(jnp.float32) * scale[pl.ds(at, 1), :]

    def summed(labels, blocks, k, want):
        value = None
        for m in range(width):
            weight = (labels[0, 0, k, m] == want).astype(jnp.float32)
            term = blocks[k * width + m].astype(jnp.float32) * weight
            value = term if value is None else value + term
        return value

    def prepare_a():
        for k in range(panel_rows):
            span = pl.ds(k * size, size)
            loads[2 * k].wait()
            for i in range(panel_rows):
                at = k * panel_rows + i
                value = summed(rows, a_in, k, i)
                coded(value, a_send, a_scale, at)
                a_high[i, :, span], a_low[i, :, span] = split(value)
                yield at

    def prepare_b():
        for k in range(panel_rows):
            span = pl.ds(k * size, size)
            loads[2 * k + 1].wait()
            for j in range(panel_rows):
                at = k * panel_rows + j
                value = summed(cols, b_in, k, j)
                coded(value, b_send, b_scale, at)
                b_high[j, span, :], b_low[j, span, :] = split(value)
                yield at

    @pl.when(early)
    def _():
        for at in prepare_b():
            if at == 0:
                await_left()
            pl.when(sends_b)(b_copy(at).start)
        pl.when(sends_b)(b_copy(groups).start)
        for at in prepare_a():
            pass

    @pl.when(late)
    def _():
        for at in prepare_a():
            pl.when(far)(a_copy(at, shift).start)
        pl.when(far)(a_copy(groups, shift).start)
        for at in prepare_b():
            pass

    @pl.when(near)
    def _():
        await_target()
        each(a_copy, "start", 0)

    @pl.when(late)
    def _():
        await_left()
        pl.when(both(sends_b, no(holds_b)))(functools.partial(each, b_copy, "start"))

    def product(i, j, ah, al, bh, bl):
        ah, al, bh, bl = ah[i], al[i], bh[j], bl[j]
        dot = lambda x, y: jnp.dot(x, y, preferred_element_type=jnp.float32)
        return dot(ah, bh) + (dot(ah, bl) + dot(al, bh) + dot(al, bl))

    kept = pattern.shape[2]
    for n in range(kept):
        block = pattern[0, 0, n]
        total[n] = product(block >> 1, block & 1, a_high, a_low, b_high, b_low)

    @pl.when(both(early, far))
    def _():
        await_target()
        pl.when(both(sends_b, holds_a))(functools.partial(each, b_copy, "wait_send"))
        each(a_copy, "start", shift)

    @pl.when(holds_b)
    def _():
        @pl.when(far)
        def _():
            each(a_copy, "wait_send", shift)
            signal(sent, up)

        @pl.when(near)
        def _():
            pl.semaphore_wait(sent, 1)

        pl.when(sends_b)(functools.partial(each, b_copy, "start"))

    def take_a(slot, high, low):
        each(a_copy, "wait_recv", slot)
        for k in range(panel_rows):
            span = pl.ds(k * size, size)
            for i in range(panel_rows):
                value = decoded(a_got.at[slot], a_scale_got.at[slot], k * panel_rows + i)
                high[i, :, span], low[i, :, span] = split(value)

    def take_b():
        each(b_copy, "wait_recv")
        for k in range(panel_rows):
            span = pl.ds(k * size, size)
            for j in range(panel_rows):
                value = decoded(b_got, b_scale_got, k * panel_rows + j)
                far_b_high[j, span, :], far_b_low[j, span, :] = split(value)

    def serve():
        take_a(1, far_a_high, far_a_low)
        for i in range(panel_rows):
            for j in range(panel_rows):
                at = i * panel_rows + j
                coded(product(i, j, far_a_high, far_a_low, b_high, b_low), c_send, c_scale, at)
                c_copy(at).start()
        c_copy(groups).start()

    pl.when(both(serves, late))(serve)

    @pl.when(both(takes_a, early))
    def _():
        take_b()
        take_a(0, a_high, a_low)

    @pl.when(both(takes_a, late))
    def _():
        take_a(0, a_high, a_low)
        take_b()

    @pl.when(takes_a)
    def _():
        for n in range(kept):
            block = pattern[0, 0, n]
            value = product(block >> 1, block & 1, a_high, a_low, far_b_high, far_b_low)
            out[0, 0, n] = (total[n] + value).astype(out.dtype)

    pl.when(both(serves, early))(serve)

    @pl.when(is_returned)
    def _():
        each(c_copy, "wait_recv")
        for n in range(kept):
            value = decoded(c_got, c_scale_got, pattern[0, 0, n])
            out[0, 0, n] = (total[n] + value).astype(out.dtype)

    @pl.when(no(both(far, holds_b)))
    def _():
        each(a_copy, "wait_send", shift)

    @pl.when(both(sends_b, no(both(far, holds_a))))
    def _():
        each(b_copy, "wait_send")

    @pl.when(serves)
    def _():
        each(c_copy, "wait_send")


def body(a_blocks, a_rows, b_blocks, b_cols, c_pattern):
    slots, size = a_blocks.shape[2], a_blocks.shape[-1]
    panel_rows = a_rows.shape[2]
    kept = c_pattern.shape[2]
    groups = panel_rows * panel_rows
    smem = pl.BlockSpec(memory_space=pltpu.SMEM)
    anywhere = pl.BlockSpec(memory_space=pl.ANY)
    bf16, f32 = jnp.bfloat16, jnp.float32
    depth = panel_rows * size
    queue = pltpu.VMEM((groups, size, size), jnp.int16)
    scale = pltpu.VMEM((8, size), f32)
    regular = pltpu.SemaphoreType.REGULAR
    sems = pltpu.SemaphoreType.DMA((groups + 1,))
    return pl.pallas_call(
        kernel,
        out_shape=jax.ShapeDtypeStruct((1, 1, kept, size, size), bf16),
        in_specs=[anywhere, smem, anywhere, smem, smem],
        out_specs=pl.BlockSpec(memory_space=pltpu.VMEM),
        scratch_shapes=[
            pltpu.VMEM((slots, size, size), bf16), pltpu.VMEM((slots, size, size), bf16),
            queue, queue, queue, pltpu.VMEM((2, groups, size, size), jnp.int16), queue, queue,
            scale, scale, scale, pltpu.VMEM((2, 8, size), f32), scale, scale,
            pltpu.VMEM((panel_rows, size, depth), bf16), pltpu.VMEM((panel_rows, size, depth), bf16),
            pltpu.VMEM((panel_rows, depth, size), bf16), pltpu.VMEM((panel_rows, depth, size), bf16),
            pltpu.VMEM((panel_rows, size, depth), bf16), pltpu.VMEM((panel_rows, size, depth), bf16),
            pltpu.VMEM((panel_rows, depth, size), bf16), pltpu.VMEM((panel_rows, depth, size), bf16),
            pltpu.VMEM((kept, size, size), f32),
            pltpu.SemaphoreType.DMA((2, panel_rows)), sems, sems, sems,
            pltpu.SemaphoreType.DMA((2, groups + 1)), sems, sems, regular, regular, regular,
        ],
        compiler_params=pltpu.CompilerParams(
            collective_id=0, has_side_effects=True, vmem_limit_bytes=60 << 20
        ),
        cost_estimate=pl.CostEstimate(flops=64 * 2 * size**3, bytes_accessed=3 << 20, transcendentals=0),
    )(a_blocks, a_rows, b_blocks, b_cols, c_pattern)


def solution(mesh):
    in_specs = (
        P("row", "col", None, None, None),
        P("row", "col", None, None),
        P("row", "col", None, None, None),
        P("row", "col", None, None),
        P("row", "col", None),
    )
    out_specs = P("row", "col", None, None, None)
    return jax.shard_map(body, mesh=mesh, in_specs=in_specs, out_specs=out_specs, check_vma=False)
```

```python
import functools

import jax
import jax.numpy as jnp
from jax import lax
from jax.experimental import pallas as pl
from jax.experimental.pallas import tpu as pltpu
from jax.sharding import PartitionSpec as P

MESH = pl.DeviceIdType.MESH
TINY = 1.2e-34
TOP = 32767.0
HOLDS = 0b10110000
BELOW_LATE = 0b11100000
LEFT_LATE = 0b10000000


def split(value):
    high = value.astype(jnp.bfloat16)
    low = (value - high.astype(jnp.float32)).astype(jnp.bfloat16)
    return high, low


def kernel(
    a_hbm, rows, b_hbm, cols, pattern, out,
    a_in, b_in, a_send, b_send, a_got, b_got,
    a_scale, b_scale, a_scale_got, b_scale_got,
    a_high, a_low, b_high, b_low, total,
    load_sem, a_send_sem, b_send_sem, a_recv_sem, b_recv_sem, below_in, left_in, sent,
):
    n_row, n_col = lax.axis_size("row"), lax.axis_size("col")
    r, c = lax.axis_index("row"), lax.axis_index("col")
    panel_rows, width = rows.shape[2], rows.shape[3]
    size = a_in.shape[-1]
    groups = panel_rows * panel_rows
    both, either, no = jnp.logical_and, jnp.logical_or, jnp.logical_not

    core, half, lane = lax.rem(r, 2), lax.rem(lax.div(r, 2), 2), lax.rem(c, 4)
    late = half == 1
    early = no(late)

    def listed(table, half, lane):
        return lax.rem(lax.shift_right_logical(table, half * 4 + lane), 2)

    near, far = core == 1, core == 0
    holds_b = both(late, listed(HOLDS, half, lane) == 1)
    holds_a = both(early, listed(HOLDS, half, lane) == 1)

    c_up, c_left = lax.rem(c + 1, n_col), lax.rem(c + n_col - 1, n_col)
    r_up = lax.rem(r + 1, n_row)
    target = (lax.rem(r + n_row - 1, n_row), c)
    up = (r_up, c)
    right, left = (r, c_up), (r, c_left)

    loads = []
    for k in range(panel_rows):
        part = pl.ds(k * width, width)
        for n, (source, into) in enumerate(((a_hbm, a_in), (b_hbm, b_in))):
            copy = pltpu.make_async_copy(source.at[0, 0, part], into.at[part], load_sem.at[n, k])
            copy.start()
            loads.append(copy)

    barrier = pltpu.get_barrier_semaphore()
    target_later = either(near, early)
    source_later = both(near, early)
    right_later, left_later = lane < 3, lane == 0

    def signal(sem, device):
        pl.semaphore_signal(sem, inc=1, device_id=device, device_id_type=MESH)

    before = 0
    for later, device in (
        (source_later, up), (target_later, target), (right_later, right), (left_later, left),
    ):
        pl.when(later)(functools.partial(signal, barrier, device))
        before = before + jnp.where(later, 0, 1)

    @pl.when(before > 0)
    def _():
        pl.semaphore_wait(barrier, before)

    def answer_below():
        pl.when(no(source_later))(functools.partial(signal, below_in, up))

    def answer_left():
        pl.when(no(right_later))(functools.partial(signal, left_in, right))

    below_waits = both(both(late, near), listed(BELOW_LATE, half, lane) == 1)
    left_waits = both(late, listed(LEFT_LATE, half, lane) == 1)
    pl.when(no(below_waits))(answer_below)
    pl.when(no(left_waits))(answer_left)

    def await_target():
        @pl.when(target_later)
        def _():
            pl.semaphore_wait(below_in, 1)

    def await_left():
        @pl.when(left_later)
        def _():
            pl.semaphore_wait(left_in, 1)

    def send(source, into, send_sem, recv_sem, device):
        return pltpu.make_async_remote_copy(
            src_ref=source, dst_ref=into, send_sem=send_sem, recv_sem=recv_sem,
            device_id=device, device_id_type=MESH,
        )

    def a_copy(at):
        sems = a_send_sem.at[at], a_recv_sem.at[at]
        if at >= groups:
            return send(a_scale.at[at - groups], a_scale_got.at[at - groups], *sems, target)
        return send(a_send.at[at], a_got.at[at], *sems, target)

    def b_copy(at):
        sems = b_send_sem.at[at], b_recv_sem.at[at]
        if at >= groups:
            return send(b_scale.at[at - groups], b_scale_got.at[at - groups], *sems, left)
        return send(b_send.at[at], b_got.at[at], *sems, left)

    def part_of(k):
        return [k * panel_rows + i for i in range(panel_rows)] + [groups + k]

    def each(copy, act, *more):
        for k in range(panel_rows):
            for at in part_of(k):
                getattr(copy(at, *more), act)()

    def coded(value, queue, scale, k, i):
        peak = jnp.maximum(jnp.max(jnp.abs(value), axis=0, keepdims=True), TINY)
        queue[k * panel_rows + i] = jnp.round(value * (TOP / peak)).astype(jnp.int32).astype(jnp.int16)
        scale[k, pl.ds(i, 1), :] = peak * (1.0 / TOP)

    def decoded(queue, scale, k, i):
        return queue[k * panel_rows + i].astype(jnp.int32).astype(jnp.float32) * scale[k, pl.ds(i, 1), :]

    def summed(labels, blocks, k, want):
        value = None
        for m in range(width):
            weight = (labels[0, 0, k, m] == want).astype(jnp.float32)
            term = blocks[k * width + m].astype(jnp.float32) * weight
            value = term if value is None else value + term
        return value

    def prepare_a():
        for k in range(panel_rows):
            span = pl.ds(k * size, size)
            loads[2 * k].wait()
            for i in range(panel_rows):
                value = summed(rows, a_in, k, i)
                coded(value, a_send, a_scale, k, i)
                a_high[i, :, span], a_low[i, :, span] = split(value)
                yield k * panel_rows + i
            yield groups + k

    def prepare_b():
        for k in range(panel_rows):
            span = pl.ds(k * size, size)
            loads[2 * k + 1].wait()
            for j in range(panel_rows):
                value = summed(cols, b_in, k, j)
                coded(value, b_send, b_scale, k, j)
                b_high[j, span, :], b_low[j, span, :] = split(value)
                yield k * panel_rows + j
            yield groups + k

    @pl.when(early)
    def _():
        for at in prepare_b():
            if at == 0:
                await_left()
            b_copy(at).start()
        for at in prepare_a():
            pass

    @pl.when(late)
    def _():
        for at in prepare_a():
            pl.when(far)(a_copy(at).start)
        for at in prepare_b():
            pass

    @pl.when(near)
    def _():
        await_target()
        each(a_copy, "start")

    @pl.when(both(late, no(holds_b)))
    def _():
        await_left()
        each(b_copy, "start")

    def product(i, j, span):
        ah, al, bh, bl = a_high[i, :, span], a_low[i, :, span], b_high[j, span, :], b_low[j, span, :]
        dot = lambda x, y: jnp.dot(x, y, preferred_element_type=jnp.float32)
        return dot(ah, bh) + (dot(ah, bl) + dot(al, bh) + dot(al, bl))

    kept = pattern.shape[2]
    for n in range(kept):
        block = pattern[0, 0, n]
        total[n] = product(block >> 1, block & 1, pl.ds(0, panel_rows * size))

    @pl.when(both(early, far))
    def _():
        await_target()
        pl.when(holds_a)(functools.partial(each, b_copy, "wait_send"))
        each(a_copy, "start")

    pl.when(below_waits)(answer_below)
    pl.when(left_waits)(answer_left)

    @pl.when(holds_b)
    def _():
        @pl.when(far)
        def _():
            each(a_copy, "wait_send")
            signal(sent, up)

        @pl.when(near)
        def _():
            pl.semaphore_wait(sent, 1)

        await_left()
        each(b_copy, "start")

    def take_a(k):
        span = pl.ds(k * size, size)
        for at in part_of(k):
            a_copy(at).wait_recv()
        for i in range(panel_rows):
            a_high[i, :, span], a_low[i, :, span] = split(decoded(a_got, a_scale_got, k, i))

    def take_b(k):
        span = pl.ds(k * size, size)
        for at in part_of(k):
            b_copy(at).wait_recv()
        for j in range(panel_rows):
            b_high[j, span, :], b_low[j, span, :] = split(decoded(b_got, b_scale_got, k, j))

    for k in range(panel_rows):
        @pl.when(early)
        def _():
            take_b(k)
            take_a(k)

        @pl.when(late)
        def _():
            take_a(k)
            take_b(k)

        for n in range(kept):
            block = pattern[0, 0, n]
            value = total[n] + product(block >> 1, block & 1, pl.ds(k * size, size))
            if k < panel_rows - 1:
                total[n] = value
            else:
                out[0, 0, n] = value.astype(out.dtype)

    @pl.when(no(both(far, holds_b)))
    def _():
        each(a_copy, "wait_send")

    @pl.when(no(both(far, holds_a)))
    def _():
        each(b_copy, "wait_send")


def body(a_blocks, a_rows, b_blocks, b_cols, c_pattern):
    slots, size = a_blocks.shape[2], a_blocks.shape[-1]
    panel_rows = a_rows.shape[2]
    kept = c_pattern.shape[2]
    groups = panel_rows * panel_rows
    smem = pl.BlockSpec(memory_space=pltpu.SMEM)
    anywhere = pl.BlockSpec(memory_space=pl.ANY)
    bf16, f32 = jnp.bfloat16, jnp.float32
    depth = panel_rows * size
    queue = pltpu.VMEM((groups, size, size), jnp.int16)
    scale = pltpu.VMEM((panel_rows, 8, size), f32)
    regular = pltpu.SemaphoreType.REGULAR
    sems = pltpu.SemaphoreType.DMA((groups + panel_rows,))
    return pl.pallas_call(
        kernel,
        out_shape=jax.ShapeDtypeStruct((1, 1, kept, size, size), bf16),
        in_specs=[anywhere, smem, anywhere, smem, smem],
        out_specs=pl.BlockSpec(memory_space=pltpu.VMEM),
        scratch_shapes=[
            pltpu.VMEM((slots, size, size), bf16), pltpu.VMEM((slots, size, size), bf16),
            queue, queue, queue, queue, scale, scale, scale, scale,
            pltpu.VMEM((panel_rows, size, depth), bf16), pltpu.VMEM((panel_rows, size, depth), bf16),
            pltpu.VMEM((panel_rows, depth, size), bf16), pltpu.VMEM((panel_rows, depth, size), bf16),
            pltpu.VMEM((kept, size, size), f32),
            pltpu.SemaphoreType.DMA((2, panel_rows)), sems, sems, sems, sems, regular, regular, regular,
        ],
        compiler_params=pltpu.CompilerParams(
            collective_id=0, has_side_effects=True, vmem_limit_bytes=60 << 20
        ),
        cost_estimate=pl.CostEstimate(flops=64 * 2 * size**3, bytes_accessed=3 << 20, transcendentals=0),
    )(a_blocks, a_rows, b_blocks, b_cols, c_pattern)


def solution(mesh):
    in_specs = (
        P("row", "col", None, None, None),
        P("row", "col", None, None),
        P("row", "col", None, None, None),
        P("row", "col", None, None),
        P("row", "col", None),
    )
    out_specs = P("row", "col", None, None, None)
    return jax.shard_map(body, mesh=mesh, in_specs=in_specs, out_specs=out_specs, check_vma=False)
```

```python
import functools

import jax
import jax.numpy as jnp
from jax import lax
from jax.experimental import pallas as pl
from jax.experimental.pallas import tpu as pltpu
from jax.sharding import PartitionSpec as P

MESH = pl.DeviceIdType.MESH
TINY = 1.2e-34
TOP = 32767.0
HOLDS = 0b10110000
BELOW_LATE = 0b11100000
LEFT_LATE = 0b10000000


def split(value):
    high = value.astype(jnp.bfloat16)
    low = (value - high.astype(jnp.float32)).astype(jnp.bfloat16)
    return high, low


def kernel(
    a_hbm, rows, b_hbm, cols, pattern, out,
    a_in, b_in, a_send, b_send, a_got, b_got,
    a_scale, b_scale, a_scale_got, b_scale_got,
    a_high, a_low, b_high, b_low, total,
    load_sem, a_send_sem, b_send_sem, a_recv_sem, b_recv_sem, below_in, left_in, sent,
):
    n_row, n_col = lax.axis_size("row"), lax.axis_size("col")
    r, c = lax.axis_index("row"), lax.axis_index("col")
    panel_rows, width = rows.shape[2], rows.shape[3]
    size = a_in.shape[-1]
    groups = panel_rows * panel_rows
    both, either, no = jnp.logical_and, jnp.logical_or, jnp.logical_not

    core, half, lane = lax.rem(r, 2), lax.rem(lax.div(r, 2), 2), lax.rem(c, 4)
    late = half == 1
    early = no(late)

    def listed(table, half, lane):
        return lax.rem(lax.shift_right_logical(table, half * 4 + lane), 2)

    near, far = core == 1, core == 0
    holds_b = both(late, listed(HOLDS, half, lane) == 1)
    holds_a = both(early, listed(HOLDS, half, lane) == 1)

    c_up, c_left = lax.rem(c + 1, n_col), lax.rem(c + n_col - 1, n_col)
    r_up = lax.rem(r + 1, n_row)
    target = (lax.rem(r + n_row - 1, n_row), c)
    up = (r_up, c)
    right, left = (r, c_up), (r, c_left)

    loads = []
    for k in range(panel_rows):
        part = pl.ds(k * width, width)
        for n, (source, into) in enumerate(((a_hbm, a_in), (b_hbm, b_in))):
            loads.append(pltpu.make_async_copy(source.at[0, 0, part], into.at[part], load_sem.at[n, k]))
    for copy in loads[0::2] + loads[1::2]:
        copy.start()

    barrier = pltpu.get_barrier_semaphore()
    target_later = either(near, early)
    source_later = both(near, early)
    right_later, left_later = lane < 3, lane == 0

    def signal(sem, device):
        pl.semaphore_signal(sem, inc=1, device_id=device, device_id_type=MESH)

    before = 0
    for later, device in (
        (source_later, up), (target_later, target), (right_later, right), (left_later, left),
    ):
        pl.when(later)(functools.partial(signal, barrier, device))
        before = before + jnp.where(later, 0, 1)

    @pl.when(before > 0)
    def _():
        pl.semaphore_wait(barrier, before)

    def answer_below():
        pl.when(no(source_later))(functools.partial(signal, below_in, up))

    def answer_left():
        pl.when(no(right_later))(functools.partial(signal, left_in, right))

    below_waits = both(both(late, near), listed(BELOW_LATE, half, lane) == 1)
    left_waits = both(late, listed(LEFT_LATE, half, lane) == 1)
    pl.when(no(below_waits))(answer_below)
    pl.when(no(left_waits))(answer_left)

    def await_target():
        @pl.when(target_later)
        def _():
            pl.semaphore_wait(below_in, 1)

    def await_left():
        @pl.when(left_later)
        def _():
            pl.semaphore_wait(left_in, 1)

    def send(source, into, send_sem, recv_sem, device):
        return pltpu.make_async_remote_copy(
            src_ref=source, dst_ref=into, send_sem=send_sem, recv_sem=recv_sem,
            device_id=device, device_id_type=MESH,
        )

    def a_copy(at):
        sems = a_send_sem.at[at], a_recv_sem.at[at]
        if at >= groups:
            return send(a_scale.at[at - groups], a_scale_got.at[at - groups], *sems, target)
        return send(a_send.at[at], a_got.at[at], *sems, target)

    def b_copy(at):
        sems = b_send_sem.at[at], b_recv_sem.at[at]
        if at >= groups:
            return send(b_scale.at[at - groups], b_scale_got.at[at - groups], *sems, left)
        return send(b_send.at[at], b_got.at[at], *sems, left)

    def part_of(k):
        return [k * panel_rows + i for i in range(panel_rows)] + [groups + k]

    def each(copy, act, *more):
        for k in range(panel_rows):
            for at in part_of(k):
                getattr(copy(at, *more), act)()

    def coded(value, queue, scale, k, i):
        peak = jnp.maximum(jnp.max(jnp.abs(value), axis=0, keepdims=True), TINY)
        queue[k * panel_rows + i] = jnp.round(value * (TOP / peak)).astype(jnp.int32).astype(jnp.int16)
        scale[k, pl.ds(i, 1), :] = peak * (1.0 / TOP)

    def decoded(queue, scale, k, i):
        return queue[k * panel_rows + i].astype(jnp.int32).astype(jnp.float32) * scale[k, pl.ds(i, 1), :]

    def summed(labels, blocks, k, want):
        value = None
        for m in range(width):
            weight = (labels[0, 0, k, m] == want).astype(jnp.float32)
            term = blocks[k * width + m].astype(jnp.float32) * weight
            value = term if value is None else value + term
        return value

    def prepare_a():
        for k in range(panel_rows):
            span = pl.ds(k * size, size)
            loads[2 * k].wait()
            for i in range(panel_rows):
                value = summed(rows, a_in, k, i)
                coded(value, a_send, a_scale, k, i)
                a_high[i, :, span], a_low[i, :, span] = split(value)
                yield k * panel_rows + i
            yield groups + k

    def prepare_b():
        for k in range(panel_rows):
            span = pl.ds(k * size, size)
            loads[2 * k + 1].wait()
            for j in range(panel_rows):
                value = summed(cols, b_in, k, j)
                coded(value, b_send, b_scale, k, j)
                b_high[j, span, :], b_low[j, span, :] = split(value)
                yield k * panel_rows + j
            yield groups + k

    @pl.when(early)
    def _():
        for at in prepare_b():
            if at == 0:
                await_left()
            b_copy(at).start()
        for at in prepare_a():
            pass

    @pl.when(late)
    def _():
        for at in prepare_a():
            pl.when(far)(a_copy(at).start)
        for at in prepare_b():
            pass

    @pl.when(near)
    def _():
        await_target()
        each(a_copy, "start")

    @pl.when(both(late, no(holds_b)))
    def _():
        await_left()
        each(b_copy, "start")

    def product(i, j, span):
        ah, al, bh, bl = a_high[i, :, span], a_low[i, :, span], b_high[j, span, :], b_low[j, span, :]
        dot = lambda x, y: jnp.dot(x, y, preferred_element_type=jnp.float32)
        return dot(ah, bh) + (dot(ah, bl) + dot(al, bh) + dot(al, bl))

    kept = pattern.shape[2]
    for n in range(kept):
        block = pattern[0, 0, n]
        total[n] = product(block >> 1, block & 1, pl.ds(0, panel_rows * size))

    @pl.when(both(early, far))
    def _():
        await_target()
        pl.when(holds_a)(functools.partial(each, b_copy, "wait_send"))
        each(a_copy, "start")

    pl.when(below_waits)(answer_below)
    pl.when(left_waits)(answer_left)

    @pl.when(holds_b)
    def _():
        @pl.when(far)
        def _():
            each(a_copy, "wait_send")
            signal(sent, up)

        @pl.when(near)
        def _():
            pl.semaphore_wait(sent, 1)

        await_left()
        each(b_copy, "start")

    def take_a(k):
        span = pl.ds(k * size, size)
        for at in part_of(k):
            a_copy(at).wait_recv()
        for i in range(panel_rows):
            a_high[i, :, span], a_low[i, :, span] = split(decoded(a_got, a_scale_got, k, i))

    def take_b(k):
        span = pl.ds(k * size, size)
        for at in part_of(k):
            b_copy(at).wait_recv()
        for j in range(panel_rows):
            b_high[j, span, :], b_low[j, span, :] = split(decoded(b_got, b_scale_got, k, j))

    for k in range(panel_rows):
        @pl.when(early)
        def _():
            take_b(k)
            take_a(k)

        @pl.when(late)
        def _():
            take_a(k)
            take_b(k)

        for n in range(kept):
            block = pattern[0, 0, n]
            value = total[n] + product(block >> 1, block & 1, pl.ds(k * size, size))
            if k < panel_rows - 1:
                total[n] = value
            else:
                out[0, 0, n] = value.astype(out.dtype)

    @pl.when(no(both(far, holds_b)))
    def _():
        each(a_copy, "wait_send")

    @pl.when(no(both(far, holds_a)))
    def _():
        each(b_copy, "wait_send")


def body(a_blocks, a_rows, b_blocks, b_cols, c_pattern):
    slots, size = a_blocks.shape[2], a_blocks.shape[-1]
    panel_rows = a_rows.shape[2]
    kept = c_pattern.shape[2]
    groups = panel_rows * panel_rows
    smem = pl.BlockSpec(memory_space=pltpu.SMEM)
    anywhere = pl.BlockSpec(memory_space=pl.ANY)
    bf16, f32 = jnp.bfloat16, jnp.float32
    depth = panel_rows * size
    queue = pltpu.VMEM((groups, size, size), jnp.int16)
    scale = pltpu.VMEM((panel_rows, 8, size), f32)
    regular = pltpu.SemaphoreType.REGULAR
    sems = pltpu.SemaphoreType.DMA((groups + panel_rows,))
    return pl.pallas_call(
        kernel,
        out_shape=jax.ShapeDtypeStruct((1, 1, kept, size, size), bf16),
        in_specs=[anywhere, smem, anywhere, smem, smem],
        out_specs=pl.BlockSpec(memory_space=pltpu.VMEM),
        scratch_shapes=[
            pltpu.VMEM((slots, size, size), bf16), pltpu.VMEM((slots, size, size), bf16),
            queue, queue, queue, queue, scale, scale, scale, scale,
            pltpu.VMEM((panel_rows, size, depth), bf16), pltpu.VMEM((panel_rows, size, depth), bf16),
            pltpu.VMEM((panel_rows, depth, size), bf16), pltpu.VMEM((panel_rows, depth, size), bf16),
            pltpu.VMEM((kept, size, size), f32),
            pltpu.SemaphoreType.DMA((2, panel_rows)), sems, sems, sems, sems, regular, regular, regular,
        ],
        compiler_params=pltpu.CompilerParams(
            collective_id=0, has_side_effects=True, vmem_limit_bytes=60 << 20
        ),
        cost_estimate=pl.CostEstimate(flops=64 * 2 * size**3, bytes_accessed=3 << 20, transcendentals=0),
    )(a_blocks, a_rows, b_blocks, b_cols, c_pattern)


def solution(mesh):
    in_specs = (
        P("row", "col", None, None, None),
        P("row", "col", None, None),
        P("row", "col", None, None, None),
        P("row", "col", None, None),
        P("row", "col", None),
    )
    out_specs = P("row", "col", None, None, None)
    return jax.shard_map(body, mesh=mesh, in_specs=in_specs, out_specs=out_specs, check_vma=False)
```
